32 devices in a mesh: mem: 8 (over z, core), space: 4 (over y, x).
Axes of the slice: x: 2, y: 2, z: 4, core: 2. Of those that a mesh axis runs over, the one named last changes fastest.
Arguments:
- yb_pert: bfloat16 [256, 16384], P('mem', 'space'), may hold values from -2.5 to 2.5
- innov: float32 [16384], P('space'), may hold values from -6 to 6
- obs_rinv: float32 [16384], P('space'), may hold values from 0.5 to 4
- obs_count: int32 [128], P('space'), may hold values from 32 to 128
- block_list: int32 [32, 4, 16], P('mem', 'space'), may hold values from -1 to 95, as said below
- loc_weight: float32 [32, 4, 16], P('mem', 'space'), may hold values from 0.1 to 1
- state: bfloat16 [256, 4, 32, 576], P('mem', 'space'), may hold values from -6 to 6
Outputs:
- analysis: bfloat16 [256, 4, 32, 576], P('mem', 'space')
The draws below stay inside these ranges and needn't reach their ends.
Inputs may be any that keep to these rules, and one draw needn't show every extreme that they name: `block_list`: each patch lists distinct blocks of its window, filled slots first then -1; a patch of the first strip lists no block of the previous strip, one of the last strip none of the next; every patch fills at least 8 slots and some patch all 16.
All inputs are finite; a program needn't handle non-finite values.
Results may differ from the reference program's by a relative error of at most 0.012.
Values may be sent and summed in bfloat16 or wider, within the bound.
A program may use at most 64 MiB of HBM per device.

```python
import math
import jax
import jax.numpy as jnp
from jax import lax

K = 256
BLOCK = 128
NB = 16
NSI = 6
OBS_BLK = 32
CELLS = 576
PATCH_COLS = 32
STRIPS = 4
BLOCKS = 128
OBS = 16384


def draw_block_list(key, part):
    key = jax.random.fold_in(key, 7)
    key_score, key_count = jax.random.split(key)
    window = 3 * OBS_BLK
    raw_score = jax.random.randint(key_score, (PATCH_COLS, STRIPS, window), 0, 1 << 20)
    block_pos = jnp.arange(window, dtype=jnp.int32)[None, None, :]
    strip_pos = jnp.arange(STRIPS, dtype=jnp.int32)[None, :, None]
    score = raw_score * window + block_pos
    barred = (strip_pos == 0) & (block_pos < OBS_BLK) | (strip_pos == STRIPS - 1) & (block_pos >= 2 * OBS_BLK)
    score = jnp.where(barred, -1, score)
    top_values, picks = lax.top_k(score, NB)
    filled = jax.random.randint(key_count, (PATCH_COLS, STRIPS, 1), NB // 2, NB + 1)
    filled = filled.at[0, 0, 0].set(NB)
    slot_pos = jnp.arange(NB, dtype=jnp.int32)[None, None, :]
    return jnp.where(slot_pos < filled, picks, -1).astype(jnp.int32)


def place_ends(drawn, key, smallest, largest):
    place = [jax.random.randint(jax.random.fold_in(key, axis), (), 0, length) for axis, length in enumerate(drawn.shape)]
    longest = drawn.shape.index(max(drawn.shape))
    neighbour = place[:longest] + [(place[longest] + 1) % drawn.shape[longest]] + place[longest + 1:]
    return drawn.at[tuple(place)].set(smallest).at[tuple(neighbour)].set(largest)


def block_scale(stream_key, dims, shards, low, top_value):
    level = 1.0
    for axis_at, shards_of in shards:
        heights = jax.random.uniform(jax.random.fold_in(jax.random.fold_in(stream_key, 6), axis_at), (shards_of,), jnp.float32, low / len(shards), top_value / len(shards))
        level = level * jnp.repeat(jnp.exp(heights), dims[axis_at] // shards_of).reshape((-1,) + (1,) * (len(dims) - 1 - axis_at))
    return level


def bell_draw(key, dims, width, reach, shards=(), kind=jnp.bfloat16):
    level = block_scale(key, dims, shards, -0.22, 0.18) if shards else 1.0
    result = jax.random.normal(key, dims, jnp.float32) * width * level
    return jnp.minimum(jnp.maximum(result, -reach), reach).astype(kind)


def setup_inputs(seed: int = 0) -> dict:
    splits = jax.random.split(jax.random.key(seed), 8)
    return {
        "yb_pert": bell_draw(splits[0], (K, OBS), 0.35, 2.5, ((0, 8), (1, 4))),
        "innov": bell_draw(splits[1], (OBS,), 1.0, 6.0, ((0, 4),), jnp.float32),
        "obs_rinv": jnp.clip(jnp.exp(math.log(4.0) - 2.0794415 * jax.random.uniform(splits[2], (OBS,), jnp.float32) ** block_scale(splits[2], (OBS,), ((0, 4),), -0.2, 0.2)), 0.5, 4.0),
        "obs_count": place_ends(jax.random.randint(splits[3], (BLOCKS,), 32, BLOCK + 1), jax.random.fold_in(splits[3], 1), 32, BLOCK).astype(jnp.int32),
        "block_list": draw_block_list(jax.random.fold_in(splits[7], 71), 0),
        "loc_weight": jnp.clip(jnp.exp(math.log(1.0) - 2.3025851 * jax.random.uniform(splits[5], (PATCH_COLS, STRIPS, NB), jnp.float32) ** block_scale(splits[5], (PATCH_COLS, STRIPS, NB), ((0, 8), (1, 4)), -0.2, 0.2)), 0.1, 1.0),
        "state": bell_draw(splits[6], (K, STRIPS, PATCH_COLS, CELLS), 1.0, 6.0, ((0, 8), (1, 4))),
    }


inflation = 1.1

def matmul_high(left, right):
    return jnp.matmul(left, right, precision=lax.Precision.HIGHEST)

def analyse(member_win, rinv_win, innov_win, slot_index, slot_loc, columns):
    members = member_win.shape[0]
    patches = slot_index.shape[0]
    slot_clip = jnp.maximum(slot_index, 0)
    slot_live = (slot_index >= 0).astype(jnp.float32)
    chosen = member_win[:, slot_clip, :]
    chosen = jnp.transpose(chosen, (1, 0, 2, 3)).reshape(patches, members, -1)
    weight_obs = rinv_win[slot_clip] * (slot_loc * slot_live)[:, :, None]
    innov_obs = innov_win[slot_clip]
    root_weight = jnp.sqrt(weight_obs).reshape(patches, -1)
    scaled = (chosen.astype(jnp.float32) * root_weight[:, None, :]).astype(jnp.bfloat16)
    scaled_f = scaled.astype(jnp.float32)
    gram_matrix = jnp.einsum('pko,pjo->pkj', scaled_f, scaled_f, precision=lax.Precision.HIGHEST)
    projected = jnp.einsum('pko,po->pk', scaled_f, root_weight * innov_obs.reshape(patches, -1), precision=lax.Precision.HIGHEST)
    identity = jnp.eye(members, dtype=jnp.float32)
    system = gram_matrix + (members - 1) / inflation * identity
    frob_norm = jnp.sqrt(lax.optimization_barrier(jnp.sum(system * system, axis=(1, 2))))
    approx_root = system / frob_norm[:, None, None]
    inverse_root = jnp.broadcast_to(identity, system.shape)
    for iteration in range(NSI):
        correction = 1.5 * identity - 0.5 * matmul_high(inverse_root, approx_root)
        approx_root = matmul_high(approx_root, correction)
        inverse_root = matmul_high(correction, inverse_root)
    inv_half = inverse_root / jnp.sqrt(frob_norm)[:, None, None]
    inner = matmul_high(inv_half, projected[:, :, None])
    mean_weight = matmul_high(inv_half, inner)[:, :, 0]
    weights = (jnp.sqrt(float(members - 1)) * inv_half + mean_weight[:, :, None]).astype(jnp.bfloat16)
    state_f32 = columns.astype(jnp.float32)
    ens_mean = lax.optimization_barrier(jnp.mean(state_f32, axis=0))
    deviation = (state_f32 - ens_mean[None]).astype(jnp.bfloat16)
    analysed = jnp.einsum('jpc,pji->ipc', deviation.astype(jnp.float32), weights.astype(jnp.float32), precision=lax.Precision.HIGHEST)
    return (analysed + ens_mean[None]).astype(jnp.bfloat16)

def reference(yb_pert, innov, obs_rinv, obs_count, block_list, loc_weight, state):
    obs_valid = (jnp.arange(BLOCK, dtype=jnp.int32)[None, :] < obs_count[:, None]).astype(jnp.float32)
    weighted = obs_rinv.reshape(BLOCKS, BLOCK) * obs_valid
    innov_blocks = innov.reshape(BLOCKS, BLOCK)
    member_blocks = yb_pert.reshape(yb_pert.shape[0], BLOCKS, BLOCK)
    member_pad = jnp.pad(member_blocks, ((0, 0), (OBS_BLK, OBS_BLK), (0, 0)))
    weight_pad = jnp.pad(weighted, ((OBS_BLK, OBS_BLK), (0, 0)))
    innov_pad = jnp.pad(innov_blocks, ((OBS_BLK, OBS_BLK), (0, 0)))

    def one_strip(strip_id):
        start = (strip_id * OBS_BLK).astype(jnp.int32)
        member_win = lax.dynamic_slice_in_dim(member_pad, start, 3 * OBS_BLK, 1)
        rinv_win = lax.dynamic_slice_in_dim(weight_pad, start, 3 * OBS_BLK, 0)
        innov_win = lax.dynamic_slice_in_dim(innov_pad, start, 3 * OBS_BLK, 0)
        slot_index = lax.dynamic_index_in_dim(block_list, strip_id, 1, keepdims=False)
        slot_loc = lax.dynamic_index_in_dim(loc_weight, strip_id, 1, keepdims=False)
        columns = lax.dynamic_index_in_dim(state, strip_id, 1, keepdims=False)
        return analyse(member_win, rinv_win, innov_win, slot_index, slot_loc, columns)
    strips_out = lax.map(one_strip, jnp.arange(STRIPS, dtype=jnp.int32))
    return jnp.transpose(strips_out, (1, 0, 2, 3))
```

```python
import functools

import jax
import jax.numpy as jnp
from jax import lax
from jax.experimental import pallas as pl
from jax.experimental.pallas import tpu as pltpu
from jax.sharding import PartitionSpec as P

BLOCK = 128
NSI = 6
MESH = pl.DeviceIdType.MESH


inflation = 1.1


def gather_window(nm, ns, yb_ref, aux_ref, win_ref, auxw_ref, local_sem, local_aux_sem,
                  sz, rz, sx, rx, sc, rc, sa, ra):
    mem = lax.axis_index("mem")
    strip = lax.axis_index("space")
    nz = nm // 2
    z, core = mem // 2, lax.rem(mem, 2)
    other = mem + 1 - 2 * core
    width = yb_ref.shape[1]

    def place(index, slot):
        return win_ref.at[index, :, pl.ds(slot * width, width)]

    def peer(step):
        return lax.rem(z + step, nz) * 2 + core

    has = (strip > 0, strip < ns - 1)
    beside = (strip - 1, strip + 1)

    barrier = pltpu.get_barrier_semaphore()
    for step in range(1, nz):
        pl.semaphore_signal(barrier, inc=1, device_id=(peer(step), strip), device_id_type=MESH)
    pl.semaphore_signal(barrier, inc=1, device_id=(other, strip), device_id_type=MESH)
    for side in range(2):
        @pl.when(has[side])
        def _():
            pl.semaphore_signal(barrier, inc=1, device_id=(mem, beside[side]), device_id_type=MESH)
    pl.semaphore_wait(barrier, nz + has[0].astype(jnp.int32) + has[1].astype(jnp.int32))

    keep = pltpu.make_async_copy(yb_ref, place(mem, 1), local_sem)
    keep_aux = pltpu.make_async_copy(aux_ref, auxw_ref.at[1], local_aux_sem)

    def along(step):
        return pltpu.make_async_remote_copy(
            yb_ref, place(mem, 1), sz.at[step], rz.at[step],
            device_id=(peer(step), strip), device_id_type=MESH)

    def across(step, side):
        index = peer(step)
        return pltpu.make_async_remote_copy(
            yb_ref if step == 0 else place(index, 1), place(index, 2 - 2 * side),
            sx.at[side, step], rx.at[side, step],
            device_id=(mem, beside[side]), device_id_type=MESH)

    def arrive(step, side):
        index = peer(step)
        spot = place(index, 2 * side)
        return pltpu.make_async_remote_copy(
            spot, spot, sx.at[1 - side, step], rx.at[1 - side, step],
            device_id=(mem, beside[side]), device_id_type=MESH)

    def arrive_along(step):
        spot = place(peer(nz - step), 1)
        return pltpu.make_async_remote_copy(
            spot, spot, sz.at[step], rz.at[step],
            device_id=(peer(nz - step), strip), device_id_type=MESH)

    def over(step, slot):
        index = peer(step)
        return pltpu.make_async_remote_copy(
            yb_ref if step == 0 and slot == 1 else place(index, slot), place(index, slot),
            sc.at[slot, step], rc.at[slot, step],
            device_id=(other, strip), device_id_type=MESH)

    def arrive_over(step, slot):
        spot = place(lax.rem(z + step, nz) * 2 + 1 - core, slot)
        return pltpu.make_async_remote_copy(
            spot, spot, sc.at[slot, step], rc.at[slot, step],
            device_id=(other, strip), device_id_type=MESH)

    def beside_aux(side):
        return pltpu.make_async_remote_copy(
            aux_ref, auxw_ref.at[2 - 2 * side], sa.at[side], ra.at[side],
            device_id=(mem, beside[side]), device_id_type=MESH)

    def arrive_aux(side):
        return pltpu.make_async_remote_copy(
            aux_ref, auxw_ref.at[2 * side], sa.at[1 - side], ra.at[1 - side],
            device_id=(mem, beside[side]), device_id_type=MESH)

    def send_across(step):
        for side in range(2):
            @pl.when(has[side])
            def _():
                across(step, side).start()

    for step in range(1, nz):
        along(step).start()
    send_across(0)
    keep.start()
    keep_aux.start()
    over(0, 1).start()
    for side in range(2):
        @pl.when(has[side])
        def _():
            beside_aux(side).start()
    order = [nz - step for step in range(1, nz)]
    for step in range(1, nz):
        arrive_along(step).wait_recv()
        send_across(nz - step)
        over(nz - step, 1).start()
    for step in [0] + order:
        for side in range(2):
            @pl.when(has[side])
            def _():
                arrive(step, side).wait_recv()
                over(step, 2 * side).start()
    keep.wait()
    keep_aux.wait()
    for step in range(1, nz):
        along(step).wait_send()
    for step in [0] + order:
        over(step, 1).wait_send()
        arrive_over(step, 1).wait_recv()
        for side in range(2):
            @pl.when(has[side])
            def _():
                across(step, side).wait_send()
                over(step, 2 * side).wait_send()
                arrive_over(step, 2 * side).wait_recv()
    for side in range(2):
        @pl.when(has[side])
        def _():
            beside_aux(side).wait_send()
            arrive_aux(side).wait_recv()


def split(value):
    high = value.astype(jnp.bfloat16)
    return high, (value - high.astype(jnp.float32)).astype(jnp.bfloat16)


def matmul_split(left, right):
    (lh, ll), (rh, rl) = left, right
    return jnp.dot(jnp.concatenate([lh, lh, ll], axis=1),
                   jnp.concatenate([rh, rl, rh], axis=0),
                   preferred_element_type=jnp.float32)


def analyse(blocks, list_ref, loc_ref, win_ref, aux_ref, col_ref, out_ref, scaled_ref):
    nm, patches, rows, cells = col_ref.shape
    members = nm * rows
    slots = list_ref.shape[1]
    identity = (lax.broadcasted_iota(jnp.int32, (members, members), 0)
                == lax.broadcasted_iota(jnp.int32, (members, members), 1)).astype(jnp.float32)
    systems, projected = [], []
    for p in range(patches):
        def slot_body(j, acc):
            q = list_ref[p, j]
            live = (q >= 0).astype(jnp.float32)
            q = jnp.where(q >= 0, q, blocks)
            strip, block = q // blocks, lax.rem(q, blocks)
            lanes = pl.ds(pl.multiple_of(q * BLOCK, BLOCK), BLOCK)
            inner = pl.ds(pl.multiple_of(block * BLOCK, BLOCK), BLOCK)
            aux = aux_ref[strip, :, inner]
            root = jnp.sqrt(aux[1:2, :] * (loc_ref[p, j] * live))
            chunk = win_ref[:, :, lanes].astype(jnp.float32).reshape(members, BLOCK)
            scaled = (chunk * root).astype(jnp.bfloat16)
            scaled_ref[p, :, pl.ds(pl.multiple_of(j * BLOCK, BLOCK), BLOCK)] = scaled
            return acc + scaled.astype(jnp.float32) * (root * aux[0:1, :])
        acc = lax.fori_loop(0, slots, slot_body, jnp.zeros((members, BLOCK), jnp.float32),
                            unroll=4)
        projected.append(jnp.sum(acc, axis=1, keepdims=True))
        scaled = scaled_ref[p]
        gram = lax.dot_general(scaled, scaled, (((1,), (1,)), ((), ())),
                               preferred_element_type=jnp.float32)
        systems.append(gram + (members - 1) / inflation * identity)
    frob = [jnp.sqrt(jnp.sum(s * s, keepdims=True)) for s in systems]
    roots = [s / f for s, f in zip(systems, frob)]
    inverse = [None] * patches
    for iteration in range(NSI):
        for p in range(patches):
            y = split(roots[p])
            if iteration == 0:
                correction = 1.5 * identity - 0.5 * roots[p]
                c = split(correction)
                inverse[p] = correction
            else:
                v = split(inverse[p])
                correction = 1.5 * identity - 0.5 * matmul_split(v, y)
                c = split(correction)
                inverse[p] = matmul_split(c, v)
            if iteration < NSI - 1:
                roots[p] = matmul_split(y, c)
    for p in range(patches):
        inv_half = inverse[p] / jnp.sqrt(frob[p])
        inner = jnp.sum(inv_half * projected[p], axis=0, keepdims=True)
        mean_weight = jnp.sum(inv_half * inner, axis=1, keepdims=True)
        weights = (jnp.sqrt(float(members - 1)) * inv_half + mean_weight).astype(jnp.bfloat16)
        state = col_ref[:, p].astype(jnp.float32).reshape(members, cells)
        ens_mean = jnp.sum(state, axis=0, keepdims=True) * (1.0 / members)
        deviation = (state - ens_mean).astype(jnp.bfloat16)
        analysed = lax.dot_general(weights, deviation, (((0,), (0,)), ((), ())),
                                   preferred_element_type=jnp.float32)
        out_ref[:, p] = (analysed + ens_mean).reshape(nm, rows, cells).astype(jnp.bfloat16)


def per_device(nm, ns, yb_pert, innov, obs_rinv, obs_count, block_list, loc_weight, state):
    blocks = obs_count.shape[0]
    rows, width = yb_pert.shape
    obs_valid = (jnp.arange(BLOCK, dtype=jnp.int32)[None, :] < obs_count[:, None]).astype(
        jnp.float32
    )
    weighted = (obs_rinv.reshape(blocks, BLOCK) * obs_valid).reshape(-1)
    paired = jnp.stack([innov, weighted])
    patches = block_list.shape[0]
    slots = block_list.shape[2]
    cells = state.shape[3]
    dma = pltpu.SemaphoreType.DMA
    nz = nm // 2
    columns = jnp.transpose(state[:, 0].reshape(rows, nm, patches, cells), (1, 2, 0, 3))
    columns = lax.all_to_all(columns, "mem", split_axis=0, concat_axis=0)
    window, auxw = pl.pallas_call(
        functools.partial(gather_window, nm, ns),
        out_shape=(jax.ShapeDtypeStruct((nm, rows, 3 * width), jnp.bfloat16),
                   jax.ShapeDtypeStruct((3, 2, width), jnp.float32)),
        in_specs=[pl.BlockSpec(memory_space=pl.ANY)] * 2,
        out_specs=[pl.BlockSpec(memory_space=pl.ANY)] * 2,
        scratch_shapes=[dma, dma, dma((nz,)), dma((nz,)), dma((2, nz)), dma((2, nz)),
                        dma((3, nz)), dma((3, nz)), dma((2,)), dma((2,))],
        compiler_params=pltpu.CompilerParams(collective_id=0, has_side_effects=True),
        cost_estimate=pl.CostEstimate(flops=0, bytes_accessed=40 << 20, transcendentals=0),
        name="gather_window",
    )(yb_pert, paired)
    members = nm * rows
    vmem = pl.BlockSpec(memory_space=pltpu.VMEM)
    smem = pl.BlockSpec(memory_space=pltpu.SMEM)
    analysed = pl.pallas_call(
        functools.partial(analyse, blocks),
        out_shape=jax.ShapeDtypeStruct(columns.shape, jnp.bfloat16),
        in_specs=[smem, smem, vmem, vmem, vmem],
        out_specs=vmem,
        scratch_shapes=[pltpu.VMEM((patches, members, slots * BLOCK), jnp.bfloat16)],
        compiler_params=pltpu.CompilerParams(vmem_limit_bytes=48 << 20),
        cost_estimate=pl.CostEstimate(flops=12 << 30, bytes_accessed=16 << 20, transcendentals=0),
        name="analyse",
    )(block_list[:, 0], loc_weight[:, 0], window, auxw, columns)
    back = lax.all_to_all(analysed, "mem", split_axis=0, concat_axis=0)
    return jnp.transpose(back, (2, 0, 1, 3)).reshape(state.shape)


def solution(mesh):
    in_specs = (
        P("mem", "space"),
        P("space"),
        P("space"),
        P("space"),
        P("mem", "space", None),
        P("mem", "space", None),
        P("mem", "space", None, None),
    )
    out_specs = P("mem", "space", None, None)
    return jax.shard_map(
        functools.partial(per_device, mesh.shape["mem"], mesh.shape["space"]),
        mesh=mesh, in_specs=in_specs, out_specs=out_specs, check_vma=False
    )
```

```python
import functools

import jax
import jax.numpy as jnp
from jax import lax
from jax.experimental import pallas as pl
from jax.experimental.pallas import tpu as pltpu
from jax.sharding import PartitionSpec as P

BLOCK = 128
NSI = 6
RELAYED = (1, 2)
MESH = pl.DeviceIdType.MESH


inflation = 1.1


def gather_window(nm, ns, yb_ref, aux_ref, cut_ref, win_ref, auxw_ref, col_ref, relay_ref,
                  local_sem, local_aux_sem, local_state_sem, sz, rz, sx, rx, sc, rc, sa, ra,
                  ss, rs, sr, rr):
    mem = lax.axis_index("mem")
    strip = lax.axis_index("space")
    nz = nm // 2
    z, core = mem // 2, lax.rem(mem, 2)
    other = mem + 1 - 2 * core
    width = yb_ref.shape[1]

    def place(index, slot):
        return win_ref.at[index, :, pl.ds(slot * width, width)]

    def peer(step):
        return lax.rem(z + step, nz) * 2 + core

    has = (strip > 0, strip < ns - 1)
    beside = (strip - 1, strip + 1)
    relayed = RELAYED if ns == 4 else ()
    inner = jnp.logical_or(strip == 1, strip == 2)
    facing = lax.rem(strip + 2, ns)

    barrier = pltpu.get_barrier_semaphore()
    for step in range(1, nm):
        pl.semaphore_signal(barrier, inc=1, device_id=(lax.rem(mem + step, nm), strip),
                            device_id_type=MESH)
    for side in range(2):
        @pl.when(has[side])
        def _():
            pl.semaphore_signal(barrier, inc=1, device_id=(mem, beside[side]), device_id_type=MESH)
    if relayed:
        pl.semaphore_signal(barrier, inc=1, device_id=(mem, facing), device_id_type=MESH)
    pl.semaphore_wait(
        barrier,
        nm - 1 + bool(relayed) + has[0].astype(jnp.int32) + has[1].astype(jnp.int32))

    keep = pltpu.make_async_copy(yb_ref, place(mem, 1), local_sem)
    keep_aux = pltpu.make_async_copy(aux_ref, auxw_ref.at[1], local_aux_sem)

    keep_state = pltpu.make_async_copy(cut_ref.at[mem], col_ref.at[mem], local_state_sem)

    def state_out(step):
        to = lax.rem(mem + step, nm)
        return pltpu.make_async_remote_copy(
            cut_ref.at[to], col_ref.at[mem], ss.at[step], rs.at[step],
            device_id=(to, strip), device_id_type=MESH)

    def state_in(step):
        source = lax.rem(mem + nm - step, nm)
        return pltpu.make_async_remote_copy(
            cut_ref.at[source], col_ref.at[source], ss.at[step], rs.at[step],
            device_id=(source, strip), device_id_type=MESH)

    def along(step):
        return pltpu.make_async_remote_copy(
            yb_ref, place(mem, 1), sz.at[step], rz.at[step],
            device_id=(peer(step), strip), device_id_type=MESH)

    def across(step, side):
        index = peer(step)
        return pltpu.make_async_remote_copy(
            yb_ref if step == 0 else place(index, 1), place(index, 2 - 2 * side),
            sx.at[side, step], rx.at[side, step],
            device_id=(mem, beside[side]), device_id_type=MESH)

    def arrive(step, side):
        index = peer(step)
        spot = place(index, 2 * side)
        return pltpu.make_async_remote_copy(
            spot, spot, sx.at[1 - side, step], rx.at[1 - side, step],
            device_id=(mem, beside[side]), device_id_type=MESH)

    def arrive_along(step):
        spot = place(peer(nz - step), 1)
        return pltpu.make_async_remote_copy(
            spot, spot, sz.at[step], rz.at[step],
            device_id=(peer(nz - step), strip), device_id_type=MESH)

    def over(step, slot):
        index = peer(step)
        return pltpu.make_async_remote_copy(
            yb_ref if step == 0 and slot == 1 else place(index, slot), place(index, slot),
            sc.at[slot, step], rc.at[slot, step],
            device_id=(other, strip), device_id_type=MESH)

    def arrive_over(step, slot):
        spot = place(lax.rem(z + step, nz) * 2 + 1 - core, slot)
        return pltpu.make_async_remote_copy(
            spot, spot, sc.at[slot, step], rc.at[slot, step],
            device_id=(other, strip), device_id_type=MESH)

    def beside_aux(side):
        return pltpu.make_async_remote_copy(
            aux_ref, auxw_ref.at[2 - 2 * side], sa.at[side], ra.at[side],
            device_id=(mem, beside[side]), device_id_type=MESH)

    def arrive_aux(side):
        return pltpu.make_async_remote_copy(
            aux_ref, auxw_ref.at[2 * side], sa.at[1 - side], ra.at[1 - side],
            device_id=(mem, beside[side]), device_id_type=MESH)

    def first_leg(step):
        index = peer(step)
        return pltpu.make_async_remote_copy(
            yb_ref if step == 0 else place(index, 1), relay_ref.at[relayed.index(step)],
            sr.at[relayed.index(step)], rr.at[relayed.index(step)],
            device_id=(mem, facing), device_id_type=MESH)

    def second_leg(step, side):
        return pltpu.make_async_remote_copy(
            relay_ref.at[relayed.index(step)], place(peer(step), 2 - 2 * side),
            sr.at[relayed.index(step)], rx.at[side, step],
            device_id=(mem, (1, 2)[side]), device_id_type=MESH)

    def direct(step, side):
        if step not in relayed:
            return has[side]
        return jnp.logical_and(has[side], strip != (2, 1)[side])

    def send_across(step):
        for side in range(2):
            @pl.when(direct(step, side))
            def _():
                across(step, side).start()
        if step in relayed:
            @pl.when(inner)
            def _():
                first_leg(step).start()

    def pass_on(step):
        if step in relayed:
            for side in range(2):
                @pl.when(strip == (0, 3)[side])
                def _():
                    first_leg(step).wait_recv()
                    second_leg(step, side).start()

    for step in range(1, nz):
        along(step).start()
    send_across(0)
    keep.start()
    keep_aux.start()
    over(0, 1).start()
    for side in range(2):
        @pl.when(has[side])
        def _():
            beside_aux(side).start()
    order = [nz - step for step in range(1, nz)]
    for step in range(1, nz):
        arrive_along(step).wait_recv()
        send_across(nz - step)
        over(nz - step, 1).start()
    for step in sorted(range(1, nm), key=lambda step: -min(step, nm - step)):
        state_out(step).start()
    keep_state.start()
    for step in [0] + order:
        pass_on(step)
        for side in range(2):
            @pl.when(has[side])
            def _():
                arrive(step, side).wait_recv()
                over(step, 2 * side).start()
    keep.wait()
    keep_aux.wait()
    keep_state.wait()
    for step in range(1, nm):
        state_out(step).wait_send()
        state_in(step).wait_recv()
    for step in range(1, nz):
        along(step).wait_send()
    for step in [0] + order:
        over(step, 1).wait_send()
        arrive_over(step, 1).wait_recv()
        if step in relayed:
            @pl.when(inner)
            def _():
                first_leg(step).wait_send()
            for side in range(2):
                @pl.when(strip == (0, 3)[side])
                def _():
                    second_leg(step, side).wait_send()
        for side in range(2):
            @pl.when(direct(step, side))
            def _():
                across(step, side).wait_send()

            @pl.when(has[side])
            def _():
                over(step, 2 * side).wait_send()
                arrive_over(step, 2 * side).wait_recv()
    for side in range(2):
        @pl.when(has[side])
        def _():
            beside_aux(side).wait_send()
            arrive_aux(side).wait_recv()


def split(value):
    high = value.astype(jnp.bfloat16)
    return high, (value - high.astype(jnp.float32)).astype(jnp.bfloat16)


def matmul_split(left, right):
    (lh, ll), (rh, rl) = left, right
    return jnp.dot(jnp.concatenate([lh, lh, ll], axis=1),
                   jnp.concatenate([rh, rl, rh], axis=0),
                   preferred_element_type=jnp.float32)


def gram_of_patches(blocks, list_ref, loc_ref, win_ref, aux_ref, system_ref, proj_ref,
                    scaled_ref):
    patches, slots = list_ref.shape
    members = system_ref.shape[1]
    identity = (lax.broadcasted_iota(jnp.int32, (members, members), 0)
                == lax.broadcasted_iota(jnp.int32, (members, members), 1)).astype(jnp.float32)
    for p in range(patches):
        def slot_body(j, acc):
            q = list_ref[p, j]
            live = (q >= 0).astype(jnp.float32)
            q = jnp.where(q >= 0, q, blocks)
            lanes = pl.ds(pl.multiple_of(q * BLOCK, BLOCK), BLOCK)
            inner = pl.ds(pl.multiple_of(lax.rem(q, blocks) * BLOCK, BLOCK), BLOCK)
            aux = aux_ref[q // blocks, :, inner]
            root = jnp.sqrt(aux[1:2, :] * (loc_ref[p, j] * live))
            chunk = win_ref[:, :, lanes].astype(jnp.float32).reshape(members, BLOCK)
            scaled = (chunk * root).astype(jnp.bfloat16)
            scaled_ref[p, :, pl.ds(pl.multiple_of(j * BLOCK, BLOCK), BLOCK)] = scaled
            return acc + scaled.astype(jnp.float32) * (root * aux[0:1, :])
        acc = lax.fori_loop(0, slots, slot_body, jnp.zeros((members, BLOCK), jnp.float32),
                            unroll=4)
        proj_ref[p] = jnp.sum(acc, axis=1, keepdims=True)
        scaled = scaled_ref[p]
        gram = lax.dot_general(scaled, scaled, (((1,), (1,)), ((), ())),
                               preferred_element_type=jnp.float32)
        system_ref[p] = gram + (members - 1) / inflation * identity


def analyse(cells, system_ref, proj_ref, col_ref, back_ref, out_ref, local_sem, send_sem,
            recv_sem):
    nm, rows, total = col_ref.shape
    patches = system_ref.shape[0]
    members = nm * rows
    group = 2
    span = group * cells
    mem, strip = lax.axis_index("mem"), lax.axis_index("space")
    barrier = pltpu.get_barrier_semaphore()
    for step in range(1, nm):
        pl.semaphore_signal(barrier, inc=1, device_id=(lax.rem(mem + step, nm), strip),
                            device_id_type=MESH)
    pl.semaphore_wait(barrier, nm - 1)
    identity = (lax.broadcasted_iota(jnp.int32, (members, members), 0)
                == lax.broadcasted_iota(jnp.int32, (members, members), 1)).astype(jnp.float32)

    def returned(first, step):
        to = lax.rem(mem + step, nm)
        lanes = pl.ds(first * cells, span)
        return pltpu.make_async_remote_copy(
            out_ref.at[to, :, lanes], back_ref.at[mem, :, lanes],
            send_sem.at[first // group, step], recv_sem.at[first // group, step],
            device_id=(to, strip), device_id_type=MESH)

    def received(first, step):
        source = lax.rem(mem + nm - step, nm)
        spot = back_ref.at[source, :, pl.ds(first * cells, span)]
        return pltpu.make_async_remote_copy(
            spot, spot, send_sem.at[first // group, step], recv_sem.at[first // group, step],
            device_id=(source, strip), device_id_type=MESH)

    steps = sorted(range(1, nm), key=lambda step: -min(step, nm - step))
    for first in range(0, patches, group):
        here = range(group)
        systems = [system_ref[first + p] for p in here]
        projected = [proj_ref[first + p] for p in here]
        frob = [jnp.sqrt(jnp.sum(s * s, keepdims=True)) for s in systems]
        roots = [s / f for s, f in zip(systems, frob)]
        inverse = [None] * group
        for iteration in range(NSI):
            for p in here:
                y = split(roots[p])
                if iteration == 0:
                    correction = 1.5 * identity - 0.5 * roots[p]
                    c = split(correction)
                    inverse[p] = correction
                else:
                    v = split(inverse[p])
                    correction = 1.5 * identity - 0.5 * matmul_split(v, y)
                    c = split(correction)
                    inverse[p] = matmul_split(c, v)
                if iteration < NSI - 1:
                    roots[p] = matmul_split(y, c)
        lanes = slice(first * cells, first * cells + span)
        state = col_ref[:, :, lanes].astype(jnp.float32).reshape(members, span)
        ens_mean = jnp.sum(state, axis=0, keepdims=True) * (1.0 / members)
        deviation = (state - ens_mean).astype(jnp.bfloat16)
        analysed = []
        for p in here:
            inv_half = inverse[p] / jnp.sqrt(frob[p])
            inner = jnp.sum(inv_half * projected[p], axis=0, keepdims=True)
            mean_weight = jnp.sum(inv_half * inner, axis=1, keepdims=True)
            weights = (jnp.sqrt(float(members - 1)) * inv_half + mean_weight).astype(jnp.bfloat16)
            analysed.append(lax.dot_general(
                weights, deviation[:, p * cells:(p + 1) * cells], (((0,), (0,)), ((), ())),
                preferred_element_type=jnp.float32))
        result = jnp.concatenate(analysed, axis=1) + ens_mean
        out_ref[:, :, lanes] = result.reshape(nm, rows, span).astype(jnp.bfloat16)
        for step in steps:
            returned(first, step).start()
    keep = pltpu.make_async_copy(out_ref.at[mem], back_ref.at[mem], local_sem)
    keep.start()
    keep.wait()
    for first in range(0, patches, group):
        for step in steps:
            returned(first, step).wait_send()
            received(first, step).wait_recv()


def per_device(nm, ns, yb_pert, innov, obs_rinv, obs_count, block_list, loc_weight, state):
    blocks = obs_count.shape[0]
    rows, width = yb_pert.shape
    obs_valid = (jnp.arange(BLOCK, dtype=jnp.int32)[None, :] < obs_count[:, None]).astype(
        jnp.float32
    )
    weighted = (obs_rinv.reshape(blocks, BLOCK) * obs_valid).reshape(-1)
    paired = jnp.stack([innov, weighted])
    patches = block_list.shape[0]
    slots = block_list.shape[2]
    cells = state.shape[3]
    dma = pltpu.SemaphoreType.DMA
    nz = nm // 2
    columns = jnp.transpose(state[:, 0].reshape(rows, nm, patches * cells), (1, 0, 2))
    window, auxw, columns, _ = pl.pallas_call(
        functools.partial(gather_window, nm, ns),
        out_shape=(jax.ShapeDtypeStruct((nm, rows, 3 * width), jnp.bfloat16),
                   jax.ShapeDtypeStruct((3, 2, width), jnp.float32),
                   jax.ShapeDtypeStruct(columns.shape, jnp.bfloat16),
                   jax.ShapeDtypeStruct((len(RELAYED), rows, width), jnp.bfloat16)),
        in_specs=[pl.BlockSpec(memory_space=pl.ANY)] * 3,
        out_specs=[pl.BlockSpec(memory_space=pl.ANY)] * 4,
        scratch_shapes=[dma, dma, dma, dma((nz,)), dma((nz,)), dma((2, nz)), dma((2, nz)),
                        dma((3, nz)), dma((3, nz)), dma((2,)), dma((2,)), dma((nm,)), dma((nm,)), dma((len(RELAYED),)),
                        dma((len(RELAYED),))],
        compiler_params=pltpu.CompilerParams(collective_id=0, has_side_effects=True),
        cost_estimate=pl.CostEstimate(flops=0, bytes_accessed=40 << 20, transcendentals=0),
        name="gather_window",
    )(yb_pert, paired, columns)
    members = nm * rows
    vmem = pl.BlockSpec(memory_space=pltpu.VMEM)
    smem = pl.BlockSpec(memory_space=pltpu.SMEM)
    systems, projected = pl.pallas_call(
        functools.partial(gram_of_patches, blocks),
        out_shape=(jax.ShapeDtypeStruct((patches, members, members), jnp.float32),
                   jax.ShapeDtypeStruct((patches, members, 1), jnp.float32)),
        in_specs=[smem, smem, vmem, vmem],
        out_specs=[vmem, vmem],
        scratch_shapes=[pltpu.VMEM((patches, members, slots * BLOCK), jnp.bfloat16)],
        compiler_params=pltpu.CompilerParams(vmem_limit_bytes=48 << 20),
        cost_estimate=pl.CostEstimate(flops=2 << 30, bytes_accessed=8 << 20, transcendentals=0),
        name="gram_of_patches",
    )(block_list[:, 0], loc_weight[:, 0], window, auxw)
    back = pl.pallas_call(
        functools.partial(analyse, cells),
        out_shape=jax.ShapeDtypeStruct(columns.shape, jnp.bfloat16),
        in_specs=[vmem, vmem, vmem],
        out_specs=pl.BlockSpec(memory_space=pl.ANY),
        scratch_shapes=[pltpu.VMEM(columns.shape, jnp.bfloat16),
                        dma, dma((patches // 2, nm)), dma((patches // 2, nm))],
        compiler_params=pltpu.CompilerParams(
            collective_id=1, has_side_effects=True, vmem_limit_bytes=48 << 20),
        cost_estimate=pl.CostEstimate(flops=8 << 30, bytes_accessed=8 << 20, transcendentals=0),
        name="analyse",
    )(systems, projected, columns)
    return jnp.transpose(back, (1, 0, 2)).reshape(state.shape)


def solution(mesh):
    in_specs = (
        P("mem", "space"),
        P("space"),
        P("space"),
        P("space"),
        P("mem", "space", None),
        P("mem", "space", None),
        P("mem", "space", None, None),
    )
    out_specs = P("mem", "space", None, None)
    return jax.shard_map(
        functools.partial(per_device, mesh.shape["mem"], mesh.shape["space"]),
        mesh=mesh, in_specs=in_specs, out_specs=out_specs, check_vma=False
    )
```

```python
import functools

import jax
import jax.numpy as jnp
from jax import lax
from jax.experimental import pallas as pl
from jax.experimental.pallas import tpu as pltpu
from jax.sharding import PartitionSpec as P

BLOCK = 128
NSI = 6
RELAYED = (1, 2)
MESH = pl.DeviceIdType.MESH


inflation = 1.1


def gather_window(nm, ns, yb_ref, aux_ref, cut_ref, win_ref, auxw_ref, col_ref, relay_ref,
                  local_sem, local_aux_sem, local_state_sem, sz, rz, sx, rx, sc, rc, sa, ra,
                  ss, rs, sr, rr):
    mem = lax.axis_index("mem")
    strip = lax.axis_index("space")
    nz = nm // 2
    z, core = mem // 2, lax.rem(mem, 2)
    other = mem + 1 - 2 * core
    width = yb_ref.shape[1]

    def place(index, slot):
        return win_ref.at[index, :, pl.ds(slot * width, width)]

    def peer(step):
        return lax.rem(z + step, nz) * 2 + core

    has = (strip > 0, strip < ns - 1)
    beside = (strip - 1, strip + 1)
    relayed = RELAYED if ns == 4 else ()
    inner = jnp.logical_or(strip == 1, strip == 2)
    facing = lax.rem(strip + 2, ns)

    barrier = pltpu.get_barrier_semaphore()
    for step in range(1, nm):
        pl.semaphore_signal(barrier, inc=1, device_id=(lax.rem(mem + step, nm), strip),
                            device_id_type=MESH)
    for side in range(2):
        @pl.when(has[side])
        def _():
            pl.semaphore_signal(barrier, inc=1, device_id=(mem, beside[side]), device_id_type=MESH)
    if relayed:
        pl.semaphore_signal(barrier, inc=1, device_id=(mem, facing), device_id_type=MESH)
    pl.semaphore_wait(
        barrier,
        nm - 1 + bool(relayed) + has[0].astype(jnp.int32) + has[1].astype(jnp.int32))

    keep = pltpu.make_async_copy(yb_ref, place(mem, 1), local_sem)
    keep_aux = pltpu.make_async_copy(aux_ref, auxw_ref.at[1], local_aux_sem)

    span = col_ref.shape[2]

    def cut(index):
        return cut_ref.at[:, pl.ds(pl.multiple_of(index * span, BLOCK), span)]

    keep_state = pltpu.make_async_copy(cut(mem), col_ref.at[mem], local_state_sem)

    def state_out(step):
        to = lax.rem(mem + step, nm)
        return pltpu.make_async_remote_copy(
            cut(to), col_ref.at[mem], ss.at[step], rs.at[step],
            device_id=(to, strip), device_id_type=MESH)

    def state_in(step):
        source = lax.rem(mem + nm - step, nm)
        return pltpu.make_async_remote_copy(
            cut(source), col_ref.at[source], ss.at[step], rs.at[step],
            device_id=(source, strip), device_id_type=MESH)

    def along(way, hop):
        sign = (1, -1)[way]
        spot = place((z - sign * hop) * 2 + core, 1)
        return pltpu.make_async_remote_copy(
            yb_ref if hop == 0 else spot, spot, sz.at[way, hop], rz.at[way, hop],
            device_id=((z + sign) * 2 + core, strip), device_id_type=MESH)

    def goes(way, hop):
        return (jnp.logical_and(z >= hop, z < nz - 1) if way == 0
                else jnp.logical_and(z + hop < nz, z > 0))

    def comes(way, hop):
        return z >= hop + 1 if way == 0 else z + hop + 1 < nz

    def across(step, side):
        index = peer(step)
        return pltpu.make_async_remote_copy(
            yb_ref if step == 0 else place(index, 1), place(index, 2 - 2 * side),
            sx.at[side, step], rx.at[side, step],
            device_id=(mem, beside[side]), device_id_type=MESH)

    def arrive(step, side):
        index = peer(step)
        spot = place(index, 2 * side)
        return pltpu.make_async_remote_copy(
            spot, spot, sx.at[1 - side, step], rx.at[1 - side, step],
            device_id=(mem, beside[side]), device_id_type=MESH)

    def arrive_along(way, hop):
        sign = (1, -1)[way]
        spot = place((z - sign * (hop + 1)) * 2 + core, 1)
        return pltpu.make_async_remote_copy(
            spot, spot, sz.at[way, hop], rz.at[way, hop],
            device_id=((z - sign) * 2 + core, strip), device_id_type=MESH)

    def over(step, slot):
        index = peer(step)
        return pltpu.make_async_remote_copy(
            yb_ref if step == 0 and slot == 1 else place(index, slot), place(index, slot),
            sc.at[slot, step], rc.at[slot, step],
            device_id=(other, strip), device_id_type=MESH)

    def arrive_over(step, slot):
        spot = place(lax.rem(z + step, nz) * 2 + 1 - core, slot)
        return pltpu.make_async_remote_copy(
            spot, spot, sc.at[slot, step], rc.at[slot, step],
            device_id=(other, strip), device_id_type=MESH)

    def beside_aux(side):
        return pltpu.make_async_remote_copy(
            aux_ref, auxw_ref.at[2 - 2 * side], sa.at[side], ra.at[side],
            device_id=(mem, beside[side]), device_id_type=MESH)

    def arrive_aux(side):
        return pltpu.make_async_remote_copy(
            aux_ref, auxw_ref.at[2 * side], sa.at[1 - side], ra.at[1 - side],
            device_id=(mem, beside[side]), device_id_type=MESH)

    def first_leg(step):
        index = peer(step)
        return pltpu.make_async_remote_copy(
            yb_ref if step == 0 else place(index, 1), relay_ref.at[relayed.index(step)],
            sr.at[relayed.index(step)], rr.at[relayed.index(step)],
            device_id=(mem, facing), device_id_type=MESH)

    def second_leg(step, side):
        return pltpu.make_async_remote_copy(
            relay_ref.at[relayed.index(step)], place(peer(step), 2 - 2 * side),
            sr.at[relayed.index(step)], rx.at[side, step],
            device_id=(mem, (1, 2)[side]), device_id_type=MESH)

    def direct(step, side):
        if step not in relayed:
            return has[side]
        return jnp.logical_and(has[side], strip != (2, 1)[side])

    def send_across(step):
        for side in range(2):
            @pl.when(direct(step, side))
            def _():
                across(step, side).start()
        if step in relayed:
            @pl.when(inner)
            def _():
                first_leg(step).start()

    def pass_on(step):
        if step in relayed:
            for side in range(2):
                @pl.when(strip == (0, 3)[side])
                def _():
                    first_leg(step).wait_recv()
                    second_leg(step, side).start()

    for way in range(2):
        @pl.when(goes(way, 0))
        def _():
            along(way, 0).start()
    send_across(0)
    keep.start()
    keep_aux.start()
    over(0, 1).start()
    for side in range(2):
        @pl.when(has[side])
        def _():
            beside_aux(side).start()
    order = sorted(range(1, nz), key=lambda step: min(step, nz - step))
    for hop in range(nz - 1):
        for way in range(2):
            if hop + 1 < nz - 1:
                onward = goes(way, hop + 1)
            step = (nz - 1 - hop, 1 + hop)[way]

            @pl.when(comes(way, hop))
            def _():
                arrive_along(way, hop).wait_recv()
                if hop + 1 < nz - 1:
                    @pl.when(onward)
                    def _():
                        along(way, hop + 1).start()
                send_across(step)
                over(step, 1).start()
    for step in sorted(range(1, nm), key=lambda step: -min(step, nm - step)):
        state_out(step).start()
    keep_state.start()
    for step in [0] + order:
        pass_on(step)
        for side in range(2):
            @pl.when(has[side])
            def _():
                arrive(step, side).wait_recv()
                over(step, 2 * side).start()
    keep.wait()
    keep_aux.wait()
    keep_state.wait()
    for step in range(1, nm):
        state_out(step).wait_send()
        state_in(step).wait_recv()
    for hop in range(nz - 1):
        for way in range(2):
            @pl.when(goes(way, hop))
            def _():
                along(way, hop).wait_send()
    for step in [0] + order:
        over(step, 1).wait_send()
        arrive_over(step, 1).wait_recv()
        if step in relayed:
            @pl.when(inner)
            def _():
                first_leg(step).wait_send()
            for side in range(2):
                @pl.when(strip == (0, 3)[side])
                def _():
                    second_leg(step, side).wait_send()
        for side in range(2):
            @pl.when(direct(step, side))
            def _():
                across(step, side).wait_send()

            @pl.when(has[side])
            def _():
                over(step, 2 * side).wait_send()
                arrive_over(step, 2 * side).wait_recv()
    for side in range(2):
        @pl.when(has[side])
        def _():
            beside_aux(side).wait_send()
            arrive_aux(side).wait_recv()


def split(value):
    high = value.astype(jnp.bfloat16)
    return high, (value - high.astype(jnp.float32)).astype(jnp.bfloat16)


def matmul_split(left, right):
    (lh, ll), (rh, rl) = left, right
    return jnp.dot(jnp.concatenate([lh, lh, ll], axis=1),
                   jnp.concatenate([rh, rl, rh], axis=0),
                   preferred_element_type=jnp.float32)


def gram_of_patches(blocks, list_ref, loc_ref, win_ref, aux_ref, system_ref, proj_ref,
                    scaled_ref):
    patches, slots = list_ref.shape
    members = system_ref.shape[1]
    identity = (lax.broadcasted_iota(jnp.int32, (members, members), 0)
                == lax.broadcasted_iota(jnp.int32, (members, members), 1)).astype(jnp.float32)
    for p in range(patches):
        def slot_body(j, acc):
            q = list_ref[p, j]
            live = (q >= 0).astype(jnp.float32)
            q = jnp.where(q >= 0, q, blocks)
            lanes = pl.ds(pl.multiple_of(q * BLOCK, BLOCK), BLOCK)
            inner = pl.ds(pl.multiple_of(lax.rem(q, blocks) * BLOCK, BLOCK), BLOCK)
            aux = aux_ref[q // blocks, :, inner]
            root = jnp.sqrt(aux[1:2, :] * (loc_ref[p, j] * live))
            chunk = win_ref[:, :, lanes].astype(jnp.float32).reshape(members, BLOCK)
            scaled = (chunk * root).astype(jnp.bfloat16)
            scaled_ref[p, :, pl.ds(pl.multiple_of(j * BLOCK, BLOCK), BLOCK)] = scaled
            return acc + scaled.astype(jnp.float32) * (root * aux[0:1, :])
        acc = lax.fori_loop(0, slots, slot_body, jnp.zeros((members, BLOCK), jnp.float32),
                            unroll=4)
        proj_ref[p] = jnp.sum(acc, axis=1, keepdims=True)
        scaled = scaled_ref[p]
        gram = lax.dot_general(scaled, scaled, (((1,), (1,)), ((), ())),
                               preferred_element_type=jnp.float32)
        system_ref[p] = gram + (members - 1) / inflation * identity


def analyse(cells, system_ref, proj_ref, col_ref, back_ref, out_ref, local_sem, send_sem,
            recv_sem):
    nm, rows, total = col_ref.shape
    patches = system_ref.shape[0]
    members = nm * rows
    group = 2
    span = group * cells
    mem, strip = lax.axis_index("mem"), lax.axis_index("space")
    barrier = pltpu.get_barrier_semaphore()
    for step in range(1, nm):
        pl.semaphore_signal(barrier, inc=1, device_id=(lax.rem(mem + step, nm), strip),
                            device_id_type=MESH)
    pl.semaphore_wait(barrier, nm - 1)
    identity = (lax.broadcasted_iota(jnp.int32, (members, members), 0)
                == lax.broadcasted_iota(jnp.int32, (members, members), 1)).astype(jnp.float32)

    def spot(index, first, length):
        start = pl.multiple_of(index * total + first * cells, BLOCK)
        return back_ref.at[:, pl.ds(start, length)]

    def returned(first, step):
        to = lax.rem(mem + step, nm)
        return pltpu.make_async_remote_copy(
            out_ref.at[to, :, pl.ds(first * cells, span)], spot(mem, first, span),
            send_sem.at[first // group, step], recv_sem.at[first // group, step],
            device_id=(to, strip), device_id_type=MESH)

    def received(first, step):
        source = lax.rem(mem + nm - step, nm)
        landed = spot(source, first, span)
        return pltpu.make_async_remote_copy(
            landed, landed, send_sem.at[first // group, step], recv_sem.at[first // group, step],
            device_id=(source, strip), device_id_type=MESH)

    steps = sorted(range(1, nm), key=lambda step: -min(step, nm - step))
    for first in range(0, patches, group):
        here = range(group)
        systems = [system_ref[first + p] for p in here]
        projected = [proj_ref[first + p] for p in here]
        frob = [jnp.sqrt(jnp.sum(s * s, keepdims=True)) for s in systems]
        roots = [s / f for s, f in zip(systems, frob)]
        inverse = [None] * group
        for iteration in range(NSI):
            for p in here:
                y = split(roots[p])
                if iteration == 0:
                    correction = 1.5 * identity - 0.5 * roots[p]
                    c = split(correction)
                    inverse[p] = correction
                else:
                    v = split(inverse[p])
                    correction = 1.5 * identity - 0.5 * matmul_split(v, y)
                    c = split(correction)
                    inverse[p] = matmul_split(c, v)
                if iteration < NSI - 1:
                    roots[p] = matmul_split(y, c)
        lanes = slice(first * cells, first * cells + span)
        state = col_ref[:, :, lanes].astype(jnp.float32).reshape(members, span)
        ens_mean = jnp.sum(state, axis=0, keepdims=True) * (1.0 / members)
        deviation = (state - ens_mean).astype(jnp.bfloat16)
        analysed = []
        for p in here:
            inv_half = inverse[p] / jnp.sqrt(frob[p])
            inner = jnp.sum(inv_half * projected[p], axis=0, keepdims=True)
            mean_weight = jnp.sum(inv_half * inner, axis=1, keepdims=True)
            weights = (jnp.sqrt(float(members - 1)) * inv_half + mean_weight).astype(jnp.bfloat16)
            analysed.append(lax.dot_general(
                weights, deviation[:, p * cells:(p + 1) * cells], (((0,), (0,)), ((), ())),
                preferred_element_type=jnp.float32))
        result = jnp.concatenate(analysed, axis=1) + ens_mean
        out_ref[:, :, lanes] = result.reshape(nm, rows, span).astype(jnp.bfloat16)
        for step in steps:
            returned(first, step).start()
    keep = pltpu.make_async_copy(out_ref.at[mem], spot(mem, 0, total), local_sem)
    keep.start()
    keep.wait()
    for first in range(0, patches, group):
        for step in steps:
            returned(first, step).wait_send()
            received(first, step).wait_recv()


def per_device(nm, ns, yb_pert, innov, obs_rinv, obs_count, block_list, loc_weight, state):
    blocks = obs_count.shape[0]
    rows, width = yb_pert.shape
    obs_valid = (jnp.arange(BLOCK, dtype=jnp.int32)[None, :] < obs_count[:, None]).astype(
        jnp.float32
    )
    weighted = (obs_rinv.reshape(blocks, BLOCK) * obs_valid).reshape(-1)
    paired = jnp.stack([innov, weighted])
    patches = block_list.shape[0]
    slots = block_list.shape[2]
    cells = state.shape[3]
    dma = pltpu.SemaphoreType.DMA
    nz = nm // 2
    flat = state.reshape(rows, nm * patches * cells)
    window, auxw, columns, _ = pl.pallas_call(
        functools.partial(gather_window, nm, ns),
        out_shape=(jax.ShapeDtypeStruct((nm, rows, 3 * width), jnp.bfloat16),
                   jax.ShapeDtypeStruct((3, 2, width), jnp.float32),
                   jax.ShapeDtypeStruct((nm, rows, patches * cells), jnp.bfloat16),
                   jax.ShapeDtypeStruct((len(RELAYED), rows, width), jnp.bfloat16)),
        in_specs=[pl.BlockSpec(memory_space=pl.ANY)] * 3,
        out_specs=[pl.BlockSpec(memory_space=pl.ANY)] * 4,
        scratch_shapes=[dma, dma, dma, dma((2, nz)), dma((2, nz)), dma((2, nz)), dma((2, nz)),
                        dma((3, nz)), dma((3, nz)), dma((2,)), dma((2,)), dma((nm,)), dma((nm,)), dma((len(RELAYED),)),
                        dma((len(RELAYED),))],
        compiler_params=pltpu.CompilerParams(collective_id=0, has_side_effects=True),
        cost_estimate=pl.CostEstimate(flops=0, bytes_accessed=40 << 20, transcendentals=0),
        name="gather_window",
    )(yb_pert, paired, flat)
    members = nm * rows
    vmem = pl.BlockSpec(memory_space=pltpu.VMEM)
    smem = pl.BlockSpec(memory_space=pltpu.SMEM)
    systems, projected = pl.pallas_call(
        functools.partial(gram_of_patches, blocks),
        out_shape=(jax.ShapeDtypeStruct((patches, members, members), jnp.float32),
                   jax.ShapeDtypeStruct((patches, members, 1), jnp.float32)),
        in_specs=[smem, smem, vmem, vmem],
        out_specs=[vmem, vmem],
        scratch_shapes=[pltpu.VMEM((patches, members, slots * BLOCK), jnp.bfloat16)],
        compiler_params=pltpu.CompilerParams(vmem_limit_bytes=48 << 20),
        cost_estimate=pl.CostEstimate(flops=2 << 30, bytes_accessed=8 << 20, transcendentals=0),
        name="gram_of_patches",
    )(block_list[:, 0], loc_weight[:, 0], window, auxw)
    back = pl.pallas_call(
        functools.partial(analyse, cells),
        out_shape=jax.ShapeDtypeStruct(flat.shape, jnp.bfloat16),
        in_specs=[vmem, vmem, vmem],
        out_specs=pl.BlockSpec(memory_space=pl.ANY),
        scratch_shapes=[pltpu.VMEM(columns.shape, jnp.bfloat16),
                        dma, dma((patches // 2, nm)), dma((patches // 2, nm))],
        compiler_params=pltpu.CompilerParams(
            collective_id=1, has_side_effects=True, vmem_limit_bytes=48 << 20),
        cost_estimate=pl.CostEstimate(flops=8 << 30, bytes_accessed=8 << 20, transcendentals=0),
        name="analyse",
    )(systems, projected, columns)
    return back.reshape(state.shape)


def solution(mesh):
    in_specs = (
        P("mem", "space"),
        P("space"),
        P("space"),
        P("space"),
        P("mem", "space", None),
        P("mem", "space", None),
        P("mem", "space", None, None),
    )
    out_specs = P("mem", "space", None, None)
    return jax.shard_map(
        functools.partial(per_device, mesh.shape["mem"], mesh.shape["space"]),
        mesh=mesh, in_specs=in_specs, out_specs=out_specs, check_vma=False
    )
```
